32 devices in a mesh: replica: 2 (over x), fsdp: 8 (over z, core), tensor: 2 (over y).
Axes of the slice: x: 2, y: 2, z: 4, core: 2. Of those that a mesh axis runs over, the one named last changes fastest.
Arguments:
- inputs: bfloat16 [4096, 1024], P(('replica', 'fsdp')), may hold values from -6 to 6
- cotangent: bfloat16 [4096, 1024], P(('replica', 'fsdp')), may hold values from -6 to 6
- norm_gains: bfloat16 [2, 1024], P(None, 'fsdp'), may hold values from 0.25 to 1.75
- head_gains: bfloat16 [2, 64], P(None, 'fsdp'), may hold values from 0.25 to 1.75
- query_weight: bfloat16 [1024, 1024], P('fsdp', 'tensor'), may hold values from -0.1875 to 0.1875
- key_weight: bfloat16 [1024, 512], P('fsdp', 'tensor'), may hold values from -0.1875 to 0.1875
- value_weight: bfloat16 [1024, 512], P('fsdp', 'tensor'), may hold values from -0.1875 to 0.1875
- out_weight: bfloat16 [1024, 1024], P('tensor', 'fsdp'), may hold values from -1 to 1
- gate_weight: bfloat16 [1024, 4608], P('fsdp', 'tensor'), may hold values from -0.1875 to 0.1875
- up_weight: bfloat16 [1024, 4608], P('fsdp', 'tensor'), may hold values from -0.1875 to 0.1875
- down_weight: bfloat16 [4608, 1024], P('tensor', 'fsdp'), may hold values from -0.09375 to 0.09375
Outputs:
- output: bfloat16 [4096, 1024], P(('replica', 'fsdp'))
- input_grad: bfloat16 [4096, 1024], P(('replica', 'fsdp'))
- norm_gains_grad: float32 [2, 1024], P(None, 'fsdp')
- head_gains_grad: float32 [2, 64], P(None, 'fsdp')
- query_grad: float32 [1024, 1024], P('fsdp', 'tensor')
- key_grad: float32 [1024, 512], P('fsdp', 'tensor')
- value_grad: float32 [1024, 512], P('fsdp', 'tensor')
- out_grad: float32 [1024, 1024], P('tensor', 'fsdp')
- gate_grad: float32 [1024, 4608], P('fsdp', 'tensor')
- up_grad: float32 [1024, 4608], P('fsdp', 'tensor')
- down_grad: float32 [4608, 1024], P('tensor', 'fsdp')
The draws below stay inside these ranges and needn't reach their ends.
All inputs are finite; a program needn't handle non-finite values.
Results may differ from the reference program's by a relative error of at most 0.02.
Values may be sent and summed in bfloat16 or wider, within the bound.
A program may use at most 128 MiB of HBM per device.

```python
import math
import jax
import jax.numpy as jnp
from jax import lax

D = 1024
H = 16
KV = 8
HD = 64
FF = 4608
LEN = 256
SEQS = 16
TOKENS = 4096


def levels(stream_key, shape, pieces, least, top_value):
    level = 1.0
    for position, blocks in pieces:
        steps = jax.random.uniform(jax.random.fold_in(jax.random.fold_in(stream_key, 6), position), (blocks,), jnp.float32, least / len(pieces), top_value / len(pieces))
        level = level * jnp.repeat(jnp.exp(steps), shape[position] // blocks).reshape((-1,) + (1,) * (len(shape) - 1 - position))
    return level


def noise(stream_key, dims, scale, bound, shards=(), held_as=jnp.bfloat16):
    values = jax.random.normal(stream_key, dims, jnp.float32) * scale
    if len(shards) > 0:
        values = levels(stream_key, dims, shards, -0.22, 0.18) * values
    return jnp.clip(values, min=-bound, max=bound).astype(held_as)


def setup_inputs(seed: int = 0) -> dict:
    key_list = jax.random.split(jax.random.key(seed), 12)
    return {
        "inputs": noise(key_list[0], (TOKENS, D), 1.0, 6.0, ((0, 16),)),
        "cotangent": noise(key_list[1], (TOKENS, D), 1.0, 6.0, ((0, 16),)),
        "norm_gains": jnp.clip(1.0 + 0.15 * jax.random.normal(key_list[2], (2, D), jnp.float32), 0.25, 1.75).astype(jnp.bfloat16),
        "head_gains": jnp.clip(1.0 + 0.15 * jax.random.normal(key_list[3], (2, HD), jnp.float32), 0.25, 1.75).astype(jnp.bfloat16),
        "query_weight": noise(key_list[4], (D, H * HD), D ** -0.5, 0.1875, ((0, 8), (1, 2))),
        "key_weight": noise(key_list[5], (D, KV * HD), D ** -0.5, 0.1875, ((0, 8), (1, 2))),
        "value_weight": noise(key_list[6], (D, KV * HD), D ** -0.5, 0.1875, ((0, 8), (1, 2))),
        "out_weight": noise(key_list[7], (H * HD, D), (H * HD // 32) ** -0.5, 1.0, ((0, 2), (1, 8))),
        "gate_weight": noise(key_list[8], (D, FF), D ** -0.5, 0.1875, ((0, 8), (1, 2))),
        "up_weight": noise(key_list[9], (D, FF), D ** -0.5, 0.1875, ((0, 8), (1, 2))),
        "down_weight": noise(key_list[10], (FF, D), FF ** -0.5, 0.09375, ((0, 2), (1, 8))),
    }


@jax.custom_vjp
def low(v):
    return lax.optimization_barrier(v.astype(jnp.bfloat16)).astype(jnp.float32)

@jax.custom_vjp
def low_back(v):
    return v

def low_keep(v):
    return (low(v), None)

def low_pass(kept, grad):
    return (grad,)

def back_keep(v):
    return (v, None)

def back_low(kept, grad):
    return (low(grad),)
low.defvjp(low_keep, low_pass)
low_back.defvjp(back_keep, back_low)
epsilon = 1e-05
rope_base = 1000000.0

def normalize(values, gain):
    return values * lax.rsqrt(lax.optimization_barrier(jnp.mean(values * values, axis=-1, keepdims=True)) + epsilon) * gain

def rope_tables(length):
    half = HD // 2
    freqs = rope_base ** (-(jnp.arange(half, dtype=jnp.float32) * 2.0 / HD))
    angles = jnp.arange(length, dtype=jnp.float32)[:, None] * freqs[None, :]
    return (jnp.cos(angles)[:, None, :], jnp.sin(angles)[:, None, :])

def rotate(values, cosine_table, sine_table):
    half = values.shape[-1] // 2
    front = values[..., :half]
    behind = values[..., half:]
    return jnp.concatenate([front * cosine_table - behind * sine_table, behind * cosine_table + front * sine_table], axis=-1)

def forward(states, norm_gains, head_gains, query_weight, key_weight, value_weight, out_weight, gate_weight, up_weight, down_weight):
    highest = lax.Precision.HIGHEST
    batch = states.shape[0]
    length = states.shape[1]
    group_size = H // KV
    cosine_table, sine_table = rope_tables(length)
    first_low = low(normalize(states, norm_gains[0]))
    queries = low_back(jnp.einsum('bld,de->ble', first_low, query_weight, precision=highest)).reshape(batch, length, H, HD)
    keys = low_back(jnp.einsum('bld,de->ble', first_low, key_weight, precision=highest)).reshape(batch, length, KV, HD)
    values = low(low_back(jnp.einsum('bld,de->ble', first_low, value_weight, precision=highest))).reshape(batch, length, KV, HD)
    queries = low(rotate(normalize(queries, head_gains[0]), cosine_table, sine_table)).reshape(batch, length, KV, group_size, HD)
    keys = low(rotate(normalize(keys, head_gains[1]), cosine_table, sine_table))
    scores = low_back(jnp.einsum('blkgd,btkd->bkglt', queries, keys, precision=highest) * (1.0 / math.sqrt(HD)))
    causal = jnp.arange(length)[:, None] >= jnp.arange(length)[None, :]
    weights_low = low(jax.nn.softmax(jnp.where(causal, scores, -1e+30), axis=-1))
    mixed = low(low_back(jnp.einsum('bkglt,btkd->blkgd', weights_low, values, precision=highest))).reshape(batch, length, H * HD)
    hidden = states + low_back(jnp.einsum('ble,ed->bld', mixed, out_weight, precision=highest))
    second_low = low(normalize(hidden, norm_gains[1]))
    gate = low_back(jnp.einsum('bld,df->blf', second_low, gate_weight, precision=highest))
    upward = low_back(jnp.einsum('bld,df->blf', second_low, up_weight, precision=highest))
    inner_low = low(jax.nn.silu(gate) * upward)
    return hidden + jnp.einsum('blf,fd->bld', inner_low, down_weight, precision=highest)

def reference(inputs, cotangent, norm_gains, head_gains, query_weight, key_weight, value_weight, out_weight, gate_weight, up_weight, down_weight):
    per_step = math.gcd(SEQS, max(1, 4096 // LEN))
    step_count = SEQS // per_step
    states = inputs.astype(jnp.float32).reshape(step_count, per_step, LEN, D)
    grads_in = cotangent.astype(jnp.float32).reshape(step_count, per_step, LEN, D)
    params = (norm_gains.astype(jnp.float32), head_gains.astype(jnp.float32), query_weight.astype(jnp.float32), key_weight.astype(jnp.float32), value_weight.astype(jnp.float32), out_weight.astype(jnp.float32), gate_weight.astype(jnp.float32), up_weight.astype(jnp.float32), down_weight.astype(jnp.float32))

    def one_step(carry, pair):
        state_group, grad_group = pair
        result, pullback = jax.vjp(forward, state_group, *params)
        grads = pullback(grad_group)
        carry = tuple((before + after for before, after in zip(carry, grads[1:])))
        return (carry, (result.astype(jnp.bfloat16), grads[0].astype(jnp.bfloat16)))
    zeros = tuple((jnp.zeros(param.shape, jnp.float32) for param in params))
    sums, (results, input_grads) = lax.scan(one_step, zeros, (states, grads_in))
    return (results.reshape(TOKENS, D), input_grads.reshape(TOKENS, D), sums[0], sums[1], sums[2], sums[3], sums[4], sums[5], sums[6], sums[7], sums[8])
```

```python
import functools
import math

import jax
import jax.numpy as jnp
from jax import lax
from jax.experimental import pallas as pl
from jax.experimental.pallas import tpu as pltpu
from jax.sharding import PartitionSpec as P

HD = 64


epsilon = 1e-05
rope_base = 1000000.0


def inverse_rms(values):
    return lax.rsqrt(jnp.mean(values * values, axis=-1, keepdims=True) + epsilon)


def norm_back(grad_normed, normed, scaling, gain):
    scaled = grad_normed * gain
    return scaling * (scaled - normed * jnp.mean(scaled * normed, axis=-1, keepdims=True))


def rope_tables(length):
    half = HD // 2
    freqs = rope_base ** (-(jnp.arange(half, dtype=jnp.float32) * 2.0 / HD))
    angles = jnp.arange(length, dtype=jnp.float32)[:, None] * freqs[None, :]
    return (jnp.cos(angles)[:, None, :], jnp.sin(angles)[:, None, :])


def rotate(values, cosine_table, sine_table):
    half = values.shape[-1] // 2
    front = values[..., :half]
    behind = values[..., half:]
    return jnp.concatenate(
        [front * cosine_table - behind * sine_table, behind * cosine_table + front * sine_table],
        axis=-1,
    )


def matmul(left, right):
    return jnp.dot(left, right, preferred_element_type=jnp.float32)


def cross_rows(left, right):
    return lax.dot_general(
        left, right, (((0,), (0,)), ((), ())), preferred_element_type=jnp.float32
    )


def cross_cols(left, right):
    return lax.dot_general(
        left, right, (((1,), (1,)), ((), ())), preferred_element_type=jnp.float32
    )


MESH = pl.DeviceIdType.MESH
vmem_bytes = 60 * 1024 * 1024


def place():
    replica = lax.axis_index("replica")
    index = lax.axis_index("fsdp")
    return replica, index, index // 2, index % 2


def greet(replica, index, line, line_size, core):
    barrier = pltpu.get_barrier_semaphore()
    other_core = index + 1 - 2 * core
    other_replica = replica + 1 - 2 * (replica % 2)
    pl.semaphore_signal(barrier, inc=1, device_id={"fsdp": other_core}, device_id_type=MESH)
    pl.semaphore_signal(barrier, inc=1, device_id={"replica": other_replica}, device_id_type=MESH)

    @pl.when(line < line_size - 1)
    def _():
        pl.semaphore_signal(barrier, inc=1, device_id={"fsdp": index + 2}, device_id_type=MESH)

    @pl.when(line > 0)
    def _():
        pl.semaphore_signal(barrier, inc=1, device_id={"fsdp": index - 2}, device_id_type=MESH)

    ends = (line == 0).astype(jnp.int32) + (line == line_size - 1).astype(jnp.int32)
    pl.semaphore_wait(barrier, 4 - ends)


def remote(source, target, send, receive, where):
    return pltpu.make_async_remote_copy(
        src_ref=source,
        dst_ref=target,
        send_sem=send,
        recv_sem=receive,
        device_id=where,
        device_id_type=MESH,
    )


def gather_kernel(line_size, pieces, *refs):
    shards, wholes, sems = refs[:pieces], refs[pieces : 2 * pieces], refs[2 * pieces :]
    own_sem, core_s, core_r, line_s, line_r, pair_s, pair_r, one_s, one_r, two_s, two_r = sems
    replica, index, line, core = place()
    half = replica % 2
    to_core = {"fsdp": index + 1 - 2 * core}
    to_pair = {"replica": replica + 1 - 2 * half}
    neighbours = ({"fsdp": index + 2}, {"fsdp": index - 2})
    may_send = (line < line_size - 1, line > 0)
    started = []

    def begin(condition, copy):
        if condition is None:
            copy.start()
        else:
            pl.when(condition)(copy.start)
        started.append((condition, copy))

    def slot(position, which_core, which_half):
        return 4 * position + 2 * which_core + which_half

    greet(replica, index, line, line_size, core)
    own_copies = []
    for p in range(pieces):
        for way in range(2):
            begin(
                may_send[way],
                remote(
                    shards[p].at[half],
                    wholes[p].at[slot(line, core, half)],
                    line_s.at[way, 0, p],
                    line_r.at[way, 0, p],
                    neighbours[way],
                ),
            )
    for p in range(pieces):
        target = wholes[p].at[pl.ds(2 * index, 2)]
        begin(None, remote(shards[p], target, core_s.at[p], core_r.at[p], to_core))
        copy = pltpu.make_async_copy(shards[p], target, own_sem.at[p])
        copy.start()
        own_copies.append(copy)

    def source_of(way, hop):
        position = line - hop if way == 0 else line + hop
        return position, (position >= 0 if way == 0 else position <= line_size - 1)

    def spread(hop):
        for p in range(pieces):
            for way in range(2):
                position, present = source_of(way, hop)
                place_here = wholes[p].at[slot(position, core, 1 - half)]
                arrival = remote(
                    place_here,
                    place_here,
                    pair_s.at[way, hop - 1, p],
                    pair_r.at[way, hop - 1, p],
                    to_pair,
                )
                pl.when(present)(arrival.wait_recv)
                begin(
                    present,
                    remote(
                        place_here,
                        place_here,
                        two_s.at[way, hop - 1, p],
                        two_r.at[way, hop - 1, p],
                        to_core,
                    ),
                )

    for hop in range(1, line_size):
        for p in range(pieces):
            for way in range(2):
                position, present = source_of(way, hop)
                block = wholes[p].at[slot(position, core, half)]
                arrival = remote(
                    block,
                    block,
                    line_s.at[way, hop - 1, p],
                    line_r.at[way, hop - 1, p],
                    neighbours[way],
                )
                pl.when(present)(arrival.wait_recv)
                if hop < line_size - 1:
                    begin(
                        jnp.logical_and(present, may_send[way]),
                        remote(
                            block,
                            block,
                            line_s.at[way, hop, p],
                            line_r.at[way, hop, p],
                            neighbours[way],
                        ),
                    )
                begin(
                    present,
                    remote(
                        block,
                        block,
                        pair_s.at[way, hop - 1, p],
                        pair_r.at[way, hop - 1, p],
                        to_pair,
                    ),
                )
                begin(
                    present,
                    remote(
                        block,
                        block,
                        one_s.at[way, hop - 1, p],
                        one_r.at[way, hop - 1, p],
                        to_core,
                    ),
                )
        if hop > 1:
            spread(hop - 1)
    spread(line_size - 1)
    for p in range(pieces):
        own_copies[p].wait()
        target = wholes[p].at[pl.ds(2 * (index + 1 - 2 * core), 2)]
        remote(target, target, core_s.at[p], core_r.at[p], to_core).wait_recv()
        for hop in range(1, line_size):
            for way in range(2):
                position, present = source_of(way, hop)
                first = wholes[p].at[slot(position, 1 - core, half)]
                second = wholes[p].at[slot(position, 1 - core, 1 - half)]
                sems_at = (way, hop - 1, p)
                pl.when(present)(
                    remote(first, first, one_s.at[sems_at], one_r.at[sems_at], to_core).wait_recv
                )
                pl.when(present)(
                    remote(second, second, two_s.at[sems_at], two_r.at[sems_at], to_core).wait_recv
                )
    for condition, copy in started:
        if condition is None:
            copy.wait_send()
        else:
            pl.when(condition)(copy.wait_send)


def gather_shards(shards):
    size = lax.axis_size("fsdp")
    line_size = size // 2
    pieces = len(shards)
    split = [shard.reshape(2, shard.shape[0] // 2, shard.shape[1]) for shard in shards]
    hops = (2, line_size - 1, pieces)
    wholes = pl.pallas_call(
        functools.partial(gather_kernel, line_size, pieces),
        out_shape=[
            jax.ShapeDtypeStruct((2 * size,) + shard.shape[1:], shard.dtype) for shard in split
        ],
        in_specs=[pl.BlockSpec(memory_space=pl.ANY)] * pieces,
        out_specs=[pl.BlockSpec(memory_space=pl.ANY)] * pieces,
        scratch_shapes=[pltpu.SemaphoreType.DMA((pieces,))] * 3
        + [pltpu.SemaphoreType.DMA(hops)] * 8,
        compiler_params=pltpu.CompilerParams(
            collective_id=0, has_side_effects=True, vmem_limit_bytes=vmem_bytes
        ),
    )(*split)
    return [whole.reshape(-1, whole.shape[2]) for whole in wholes]


def reduce_kernel(line_size, pieces, *refs):
    parts, sums = refs[:pieces], refs[pieces : 2 * pieces]
    core_bufs = refs[2 * pieces : 3 * pieces]
    pair_bufs = refs[3 * pieces : 4 * pieces]
    line_bufs = refs[4 * pieces : 5 * pieces]
    last_bufs = refs[5 * pieces : 6 * pieces]
    core_s, core_r, pair_s, pair_r, line_s, line_r, last_r, end_s, end_r = refs[6 * pieces :]
    replica, index, line, core = place()
    half = replica % 2
    to_core = {"fsdp": index + 1 - 2 * core}
    to_pair = {"replica": replica + 1 - 2 * half}
    right, left = {"fsdp": index + 2}, {"fsdp": index - 2}
    order = []
    for step in range((line_size + 1) // 2):
        order.append(line_size - 1 - step)
        if step != line_size - 1 - step:
            order.append(step)
    started = []

    def begin(condition, copy):
        if condition is None:
            copy.start()
        else:
            pl.when(condition)(copy.start)
        started.append((condition, copy))

    greet(replica, index, line, line_size, core)
    for s in order:
        for p in range(pieces):
            begin(
                None,
                remote(
                    parts[p].at[pl.ds(4 * s + 2 * (1 - core), 2)],
                    core_bufs[p].at[s],
                    core_s.at[s, p],
                    core_r.at[s, p],
                    to_core,
                ),
            )
    for s in order:
        for p in range(pieces):
            arrived = core_bufs[p].at[s]
            remote(arrived, arrived, core_s.at[s, p], core_r.at[s, p], to_core).wait_recv()
            core_bufs[p][s, 1 - half] = (
                core_bufs[p][s, 1 - half] + parts[p][4 * s + 2 * core + 1 - half]
            )
            begin(
                None,
                remote(
                    core_bufs[p].at[s, 1 - half],
                    pair_bufs[p].at[s],
                    pair_s.at[s, p],
                    pair_r.at[s, p],
                    to_pair,
                ),
            )
            core_bufs[p][s, half] = core_bufs[p][s, half] + parts[p][4 * s + 2 * core + half]
    for s in order:
        for p in range(pieces):
            arrived = pair_bufs[p].at[s]
            remote(arrived, arrived, pair_s.at[s, p], pair_r.at[s, p], to_pair).wait_recv()
            pair_bufs[p][s] = pair_bufs[p][s] + core_bufs[p][s, half]
            from_line = line_bufs[p].at[s]
            passes = jnp.logical_or(
                jnp.logical_and(line < s, line > 0),
                jnp.logical_and(line > s, line < line_size - 1),
            )

            @pl.when(passes)
            def _(s=s, p=p, from_line=from_line):
                remote(
                    from_line, from_line, line_s.at[s, p], line_r.at[s, p], right
                ).wait_recv()
                pair_bufs[p][s] = pair_bufs[p][s] + line_bufs[p][s]

            begin(
                line < s,
                remote(
                    pair_bufs[p].at[s], from_line, line_s.at[s, p], line_r.at[s, p], right
                ),
            )
            begin(
                line > s + 1,
                remote(pair_bufs[p].at[s], from_line, line_s.at[s, p], line_r.at[s, p], left),
            )
            begin(
                line == s + 1,
                remote(
                    pair_bufs[p].at[s], last_bufs[p], line_s.at[s, p], last_r.at[p], left
                ),
            )
    for s in order:

        @pl.when(line == s)
        def _(s=s):
            for p in range(pieces):
                if s > 0:
                    from_line = line_bufs[p].at[s]
                    remote(
                        from_line, from_line, line_s.at[s, p], line_r.at[s, p], right
                    ).wait_recv()
                    pair_bufs[p][s] = pair_bufs[p][s] + line_bufs[p][s]
                if s < line_size - 1:
                    last = last_bufs[p]
                    remote(last, last, line_s.at[s, p], last_r.at[p], left).wait_recv()
                    pair_bufs[p][s] = pair_bufs[p][s] + last[...]
                sums[p][half] = pair_bufs[p][s]
                remote(
                    sums[p].at[half], sums[p].at[half], end_s.at[p], end_r.at[p], to_pair
                ).start()

    for p in range(pieces):
        remote(
            sums[p].at[1 - half], sums[p].at[1 - half], end_s.at[p], end_r.at[p], to_pair
        ).wait_recv()
        remote(
            sums[p].at[half], sums[p].at[half], end_s.at[p], end_r.at[p], to_pair
        ).wait_send()
    for condition, copy in started:
        if condition is None:
            copy.wait_send()
        else:
            pl.when(condition)(copy.wait_send)


def reduce_parts(parts):
    size = lax.axis_size("fsdp")
    line_size = size // 2
    pieces = len(parts)
    split = [part.reshape(2 * size, -1, part.shape[1]) for part in parts]
    blocks = [part.shape[1:] for part in split]
    kind = jnp.bfloat16
    sums = pl.pallas_call(
        functools.partial(reduce_kernel, line_size, pieces),
        out_shape=[jax.ShapeDtypeStruct((2,) + block, kind) for block in blocks],
        in_specs=[pl.BlockSpec(memory_space=pltpu.VMEM)] * pieces,
        out_specs=[pl.BlockSpec(memory_space=pltpu.VMEM)] * pieces,
        scratch_shapes=[pltpu.VMEM((line_size, 2) + block, kind) for block in blocks]
        + [pltpu.VMEM((line_size,) + block, kind) for block in blocks]
        + [pltpu.VMEM((line_size,) + block, kind) for block in blocks]
        + [pltpu.VMEM(block, kind) for block in blocks]
        + [pltpu.SemaphoreType.DMA((line_size, pieces))] * 6
        + [pltpu.SemaphoreType.DMA((pieces,))] * 3,
        compiler_params=pltpu.CompilerParams(
            collective_id=1, has_side_effects=True, vmem_limit_bytes=vmem_bytes
        ),
    )(*split)
    return [total.reshape(-1, total.shape[2]) for total in sums]


def local(
    inputs,
    cotangent,
    norm_gains,
    head_gains,
    query_weight,
    key_weight,
    value_weight,
    out_weight,
    gate_weight,
    up_weight,
    down_weight,
):
    length = inputs.shape[0]
    devices = lax.axis_size("fsdp")
    rows = query_weight.shape[0]
    head_rows = head_gains.shape[1]
    small = jnp.concatenate(
        [norm_gains.T, jnp.pad(head_gains.T, ((0, rows - head_rows), (0, 0)))], axis=1
    )
    attention_shard = jnp.concatenate(
        [query_weight, key_weight, value_weight, out_weight.T, jnp.pad(small, ((0, 0), (0, 124)))],
        axis=1,
    )
    attention_full, gate_full, up_full, down_full = gather_shards(
        [attention_shard, gate_weight, up_weight, down_weight.T]
    )
    marks = [query_weight.shape[1], key_weight.shape[1], value_weight.shape[1], out_weight.shape[0]]
    marks = [sum(marks[: at + 1]) for at in range(4)]
    query_full = attention_full[:, : marks[0]]
    key_full = attention_full[:, marks[0] : marks[1]]
    value_full = attention_full[:, marks[1] : marks[2]]
    out_full = attention_full[:, marks[2] : marks[3]]
    gains_full = attention_full[:, marks[3] : marks[3] + 2].T
    heads_full = (
        attention_full[:, marks[3] + 2 : marks[3] + 4]
        .reshape(devices, rows, 2)[:, :head_rows]
        .reshape(HD, 2)
        .T
    )
    cosine_table, sine_table = rope_tables(length)
    local_heads = query_full.shape[1] // HD
    local_groups = key_full.shape[1] // HD
    group_size = local_heads // local_groups
    block_rows = min(length, 512)
    score_scale = 1.0 / math.sqrt(HD)
    residual_in = inputs.astype(jnp.float32)
    first_scale = inverse_rms(residual_in)
    first_hat = residual_in * first_scale
    first_gain = gains_full[0].astype(jnp.float32)
    first_low = (first_hat * first_gain).astype(jnp.bfloat16)
    query_raw = matmul(first_low, query_full).reshape(length, local_heads, HD)
    key_raw = matmul(first_low, key_full).reshape(length, local_groups, HD)
    value_low = matmul(first_low, value_full).astype(jnp.bfloat16).reshape(length, local_groups, HD)
    query_gain = heads_full[0].astype(jnp.float32)
    key_gain = heads_full[1].astype(jnp.float32)
    query_scale = inverse_rms(query_raw)
    query_hat = query_raw * query_scale
    query_low = rotate(query_hat * query_gain, cosine_table, sine_table).astype(jnp.bfloat16)
    query_low = query_low.reshape(length, local_groups, group_size, HD)
    key_scale = inverse_rms(key_raw)
    key_hat = key_raw * key_scale
    key_low = rotate(key_hat * key_gain, cosine_table, sine_table).astype(jnp.bfloat16)

    def masked_scores(block_start):
        key_span = block_start + block_rows
        scores = (
            jnp.einsum("qkgd,tkd->kgqt", query_low, key_low, preferred_element_type=jnp.float32)
            * score_scale
        )
        causal = (block_start + jnp.arange(block_rows))[:, None] >= jnp.arange(key_span)[None, :]
        return jnp.where(causal, scores, -1e30)

    block_index = 0
    block_start = block_index * block_rows
    masked = masked_scores(block_start)
    highest = jnp.max(masked, axis=-1, keepdims=True)
    powers = jnp.exp(masked - highest)
    totals = jnp.sum(powers, axis=-1, keepdims=True)
    softmax_low = (powers / totals).astype(jnp.bfloat16)
    log_totals = [highest + jnp.log(totals)]
    mixed_parts = jnp.einsum(
        "kgqt,tkd->qkgd", softmax_low, value_low, preferred_element_type=jnp.float32
    )
    mixed_low = mixed_parts.astype(jnp.bfloat16).reshape(length, local_heads * HD)
    attention_total = lax.psum(cross_cols(mixed_low, out_full), "tensor")
    hidden = residual_in + attention_total
    second_scale = inverse_rms(hidden)
    second_hat = hidden * second_scale
    second_gain = gains_full[1].astype(jnp.float32)
    second_low = (second_hat * second_gain).astype(jnp.bfloat16)
    gate_value = matmul(second_low, gate_full)
    up_value = matmul(second_low, up_full)
    sigmoid_gate = jax.nn.sigmoid(gate_value)
    swish = gate_value * sigmoid_gate
    inner_low = (swish * up_value).astype(jnp.bfloat16)
    swiglu_total = lax.psum(cross_cols(inner_low, down_full).astype(jnp.bfloat16), "tensor").astype(
        jnp.float32
    )
    output = (hidden + swiglu_total).astype(jnp.bfloat16)
    grad_inner = matmul(cotangent, down_full)
    grad_gate = (
        grad_inner * up_value * sigmoid_gate * (1.0 + gate_value * (1.0 - sigmoid_gate))
    ).astype(jnp.bfloat16)
    grad_up = (grad_inner * swish).astype(jnp.bfloat16)
    grad_second = lax.psum(
        (cross_cols(grad_gate, gate_full) + cross_cols(grad_up, up_full)).astype(jnp.bfloat16),
        "tensor",
    ).astype(jnp.float32)
    second_gain_grad = jnp.sum(grad_second * second_hat, axis=0)
    grad_hidden = cotangent.astype(jnp.float32) + norm_back(
        grad_second, second_hat, second_scale, second_gain
    )
    grad_hidden_low = grad_hidden.astype(jnp.bfloat16)
    out_part = cross_rows(grad_hidden_low, mixed_low)
    grad_mixed = (
        matmul(grad_hidden_low, out_full)
        .astype(jnp.bfloat16)
        .reshape(length, local_groups, group_size, HD)
    )
    grad_keys = jnp.zeros((length, local_groups, HD), jnp.float32)
    grad_values = jnp.zeros((length, local_groups, HD), jnp.float32)
    block_index = 0
    block_start = block_index * block_rows
    key_span = block_start + block_rows
    masked = masked_scores(block_start)
    powers = jnp.exp(masked - log_totals[block_index])
    grad_powers = jnp.einsum(
        "qkgd,tkd->kgqt", grad_mixed, value_low, preferred_element_type=jnp.float32
    )
    centred = jnp.sum(powers * grad_powers, axis=-1, keepdims=True)
    grad_scores = (powers * (grad_powers - centred)).astype(jnp.bfloat16)
    query_parts = (
        jnp.einsum("kgqt,tkd->qkgd", grad_scores, key_low, preferred_element_type=jnp.float32)
        * score_scale
    )
    grad_keys = grad_keys.at[:key_span].add(
        jnp.einsum("kgqt,qkgd->tkd", grad_scores, query_low, preferred_element_type=jnp.float32)
        * score_scale
    )
    grad_values = grad_values.at[:key_span].add(
        jnp.einsum(
            "kgqt,qkgd->tkd",
            powers.astype(jnp.bfloat16),
            grad_mixed,
            preferred_element_type=jnp.float32,
        )
    )
    grad_query_rot = query_parts.reshape(length, local_heads, HD)
    grad_query_gained = rotate(grad_query_rot, cosine_table, -sine_table)
    query_gain_grad = jnp.sum(grad_query_gained * query_hat, axis=(0, 1))
    grad_query = norm_back(grad_query_gained, query_hat, query_scale, query_gain).astype(
        jnp.bfloat16
    )
    grad_query = grad_query.reshape(length, local_heads * HD)
    grad_key_gained = rotate(grad_keys, cosine_table, -sine_table)
    key_gain_grad = jnp.sum(grad_key_gained * key_hat, axis=(0, 1))
    grad_key = norm_back(grad_key_gained, key_hat, key_scale, key_gain).astype(jnp.bfloat16)
    grad_key = grad_key.reshape(length, local_groups * HD)
    grad_value = grad_values.astype(jnp.bfloat16).reshape(length, local_groups * HD)
    query_part = cross_rows(first_low, grad_query)
    key_part = cross_rows(first_low, grad_key)
    value_part = cross_rows(first_low, grad_value)
    first_part = (
        cross_cols(grad_query, query_full)
        + cross_cols(grad_key, key_full)
        + cross_cols(grad_value, value_full)
    )
    grad_first, head_part = (
        lax.psum(first_part.astype(jnp.bfloat16), "tensor").astype(jnp.float32),
        lax.psum(jnp.stack([query_gain_grad, key_gain_grad]).astype(jnp.bfloat16), "tensor").astype(
            jnp.float32
        ),
    )
    first_gain_grad = jnp.sum(grad_first * first_hat, axis=0)
    input_grad = (grad_hidden + norm_back(grad_first, first_hat, first_scale, first_gain)).astype(
        jnp.bfloat16
    )
    gains_part = jnp.stack([first_gain_grad, second_gain_grad])
    heads_part = jnp.pad(
        head_part.T.reshape(devices, head_rows, 2), ((0, 0), (0, rows - head_rows), (0, 0))
    ).reshape(devices * rows, 2)
    small_part = jnp.pad(jnp.concatenate([gains_part.T, heads_part], axis=1), ((0, 0), (0, 124)))
    attention_part = jnp.concatenate(
        [query_part, key_part, value_part, out_part, small_part], axis=1
    ).astype(jnp.bfloat16)
    summed = reduce_parts(
        [
            cross_rows(second_low, grad_gate).astype(jnp.bfloat16),
            cross_rows(second_low, grad_up).astype(jnp.bfloat16),
            cross_rows(cotangent, inner_low).astype(jnp.bfloat16),
            attention_part,
        ]
    )
    replicas = lax.axis_size("replica")
    if replicas > 2:
        summed = [lax.psum(total, "replica") * 0.5 for total in summed]
    gate_grad, up_grad, down_grad, attention_grad = [total.astype(jnp.float32) for total in summed]
    return (
        output,
        input_grad,
        attention_grad[:, marks[3] : marks[3] + 2].T,
        attention_grad[:head_rows, marks[3] + 2 : marks[3] + 4].T,
        attention_grad[:, : marks[0]],
        attention_grad[:, marks[0] : marks[1]],
        attention_grad[:, marks[1] : marks[2]],
        attention_grad[:, marks[2] : marks[3]].T,
        gate_grad,
        up_grad,
        down_grad.T,
    )


def solution(mesh):
    return jax.shard_map(
        local,
        mesh=mesh,
        in_specs=(
            P(("replica", "fsdp"), None),
            P(("replica", "fsdp"), None),
            P(None, "fsdp"),
            P(None, "fsdp"),
            P("fsdp", "tensor"),
            P("fsdp", "tensor"),
            P("fsdp", "tensor"),
            P("tensor", "fsdp"),
            P("fsdp", "tensor"),
            P("fsdp", "tensor"),
            P("tensor", "fsdp"),
        ),
        out_specs=(
            P(("replica", "fsdp"), None),
            P(("replica", "fsdp"), None),
            P(None, "fsdp"),
            P(None, "fsdp"),
            P("fsdp", "tensor"),
            P("fsdp", "tensor"),
            P("fsdp", "tensor"),
            P("tensor", "fsdp"),
            P("fsdp", "tensor"),
            P("fsdp", "tensor"),
            P("tensor", "fsdp"),
        ),
        check_vma=False,
    )
```

```python
import functools
import math

import jax
import jax.numpy as jnp
from jax import lax
from jax.experimental import pallas as pl
from jax.experimental.pallas import tpu as pltpu
from jax.sharding import PartitionSpec as P

HD = 64


epsilon = 1e-05
rope_base = 1000000.0


def inverse_rms(values):
    return lax.rsqrt(jnp.mean(values * values, axis=-1, keepdims=True) + epsilon)


def norm_back(grad_normed, normed, scaling, gain):
    scaled = grad_normed * gain
    return scaling * (scaled - normed * jnp.mean(scaled * normed, axis=-1, keepdims=True))


def rope_tables(length):
    half = HD // 2
    freqs = rope_base ** (-(jnp.arange(half, dtype=jnp.float32) * 2.0 / HD))
    angles = jnp.arange(length, dtype=jnp.float32)[:, None] * freqs[None, :]
    return (jnp.cos(angles)[:, None, :], jnp.sin(angles)[:, None, :])


def rotate(values, cosine_table, sine_table):
    half = values.shape[-1] // 2
    front = values[..., :half]
    behind = values[..., half:]
    return jnp.concatenate(
        [front * cosine_table - behind * sine_table, behind * cosine_table + front * sine_table],
        axis=-1,
    )


def matmul(left, right):
    return jnp.dot(left, right, preferred_element_type=jnp.float32)


def cross_rows(left, right):
    return lax.dot_general(
        left, right, (((0,), (0,)), ((), ())), preferred_element_type=jnp.float32
    )


def cross_cols(left, right):
    return lax.dot_general(
        left, right, (((1,), (1,)), ((), ())), preferred_element_type=jnp.float32
    )


MESH = pl.DeviceIdType.MESH
vmem_bytes = 60 * 1024 * 1024


def place():
    replica = lax.axis_index("replica")
    index = lax.axis_index("fsdp")
    return replica, index, index // 2, index % 2


def greet(replica, index, line, line_size, core):
    barrier = pltpu.get_barrier_semaphore()
    other_core = index + 1 - 2 * core
    other_replica = replica + 1 - 2 * (replica % 2)
    pl.semaphore_signal(barrier, inc=1, device_id={"fsdp": other_core}, device_id_type=MESH)
    pl.semaphore_signal(barrier, inc=1, device_id={"replica": other_replica}, device_id_type=MESH)

    @pl.when(line < line_size - 1)
    def _():
        pl.semaphore_signal(barrier, inc=1, device_id={"fsdp": index + 2}, device_id_type=MESH)

    @pl.when(line > 0)
    def _():
        pl.semaphore_signal(barrier, inc=1, device_id={"fsdp": index - 2}, device_id_type=MESH)

    ends = (line == 0).astype(jnp.int32) + (line == line_size - 1).astype(jnp.int32)
    pl.semaphore_wait(barrier, 4 - ends)


def remote(source, target, send, receive, where):
    return pltpu.make_async_remote_copy(
        src_ref=source,
        dst_ref=target,
        send_sem=send,
        recv_sem=receive,
        device_id=where,
        device_id_type=MESH,
    )


def pair_permute(values, axis):
    return lax.ppermute(values, axis, [(at, at ^ 1) for at in range(lax.axis_size(axis))])


def tensor_sum(values):
    low = values.astype(jnp.bfloat16)
    if lax.axis_size("tensor") != 2:
        return lax.psum(low.astype(jnp.float32), "tensor")
    other = pair_permute(low, "tensor")
    return low.astype(jnp.float32) + other.astype(jnp.float32)


def gather_kernel(line_size, pieces, *refs):
    shards, wholes, sems = refs[:pieces], refs[pieces : 2 * pieces], refs[2 * pieces :]
    own_sem, core_s, core_r, line_s, line_r, pair_s, pair_r, one_s, one_r, two_s, two_r = sems
    replica, index, line, core = place()
    half = replica % 2
    to_core = {"fsdp": index + 1 - 2 * core}
    to_pair = {"replica": replica + 1 - 2 * half}
    neighbours = ({"fsdp": index + 2}, {"fsdp": index - 2})
    may_send = (line < line_size - 1, line > 0)
    started = []

    def begin(condition, copy):
        if condition is None:
            copy.start()
        else:
            pl.when(condition)(copy.start)
        started.append((condition, copy))

    def slot(position, which_core, which_half):
        return 4 * position + 2 * which_core + which_half

    greet(replica, index, line, line_size, core)
    own_copies = []
    for p in range(pieces):
        for way in range(2):
            begin(
                may_send[way],
                remote(
                    shards[p].at[half],
                    wholes[p].at[slot(line, core, half)],
                    line_s.at[way, 0, p],
                    line_r.at[way, 0, p],
                    neighbours[way],
                ),
            )
    for p in range(pieces):
        target = wholes[p].at[pl.ds(2 * index, 2)]
        begin(None, remote(shards[p], target, core_s.at[p], core_r.at[p], to_core))
        copy = pltpu.make_async_copy(shards[p], target, own_sem.at[p])
        copy.start()
        own_copies.append(copy)

    def source_of(way, hop):
        position = line - hop if way == 0 else line + hop
        return position, (position >= 0 if way == 0 else position <= line_size - 1)

    def spread(hop):
        for p in range(pieces):
            for way in range(2):
                position, present = source_of(way, hop)
                place_here = wholes[p].at[slot(position, core, 1 - half)]
                arrival = remote(
                    place_here,
                    place_here,
                    pair_s.at[way, hop - 1, p],
                    pair_r.at[way, hop - 1, p],
                    to_pair,
                )
                pl.when(present)(arrival.wait_recv)
                begin(
                    present,
                    remote(
                        place_here,
                        place_here,
                        two_s.at[way, hop - 1, p],
                        two_r.at[way, hop - 1, p],
                        to_core,
                    ),
                )

    for hop in range(1, line_size):
        for p in range(pieces):
            for way in range(2):
                position, present = source_of(way, hop)
                block = wholes[p].at[slot(position, core, half)]
                arrival = remote(
                    block,
                    block,
                    line_s.at[way, hop - 1, p],
                    line_r.at[way, hop - 1, p],
                    neighbours[way],
                )
                pl.when(present)(arrival.wait_recv)
                if hop < line_size - 1:
                    begin(
                        jnp.logical_and(present, may_send[way]),
                        remote(
                            block,
                            block,
                            line_s.at[way, hop, p],
                            line_r.at[way, hop, p],
                            neighbours[way],
                        ),
                    )
                begin(
                    present,
                    remote(
                        block,
                        block,
                        pair_s.at[way, hop - 1, p],
                        pair_r.at[way, hop - 1, p],
                        to_pair,
                    ),
                )
                begin(
                    present,
                    remote(
                        block,
                        block,
                        one_s.at[way, hop - 1, p],
                        one_r.at[way, hop - 1, p],
                        to_core,
                    ),
                )
        if hop > 1:
            spread(hop - 1)
    spread(line_size - 1)
    for p in range(pieces):
        own_copies[p].wait()
        target = wholes[p].at[pl.ds(2 * (index + 1 - 2 * core), 2)]
        remote(target, target, core_s.at[p], core_r.at[p], to_core).wait_recv()
        for hop in range(1, line_size):
            for way in range(2):
                position, present = source_of(way, hop)
                first = wholes[p].at[slot(position, 1 - core, half)]
                second = wholes[p].at[slot(position, 1 - core, 1 - half)]
                sems_at = (way, hop - 1, p)
                pl.when(present)(
                    remote(first, first, one_s.at[sems_at], one_r.at[sems_at], to_core).wait_recv
                )
                pl.when(present)(
                    remote(second, second, two_s.at[sems_at], two_r.at[sems_at], to_core).wait_recv
                )
    for condition, copy in started:
        if condition is None:
            copy.wait_send()
        else:
            pl.when(condition)(copy.wait_send)


def gather_shards(shards):
    size = lax.axis_size("fsdp")
    line_size = size // 2
    pieces = len(shards)
    split = [shard.reshape(2, shard.shape[0] // 2, shard.shape[1]) for shard in shards]
    hops = (2, line_size - 1, pieces)
    wholes = pl.pallas_call(
        functools.partial(gather_kernel, line_size, pieces),
        out_shape=[
            jax.ShapeDtypeStruct((2 * size,) + shard.shape[1:], shard.dtype) for shard in split
        ],
        in_specs=[pl.BlockSpec(memory_space=pl.ANY)] * pieces,
        out_specs=[pl.BlockSpec(memory_space=pl.ANY)] * pieces,
        scratch_shapes=[pltpu.SemaphoreType.DMA((pieces,))] * 3
        + [pltpu.SemaphoreType.DMA(hops)] * 8,
        compiler_params=pltpu.CompilerParams(
            collective_id=0, has_side_effects=True, vmem_limit_bytes=vmem_bytes
        ),
    )(*split)
    return [whole.reshape(-1, whole.shape[2]) for whole in wholes]


def reduce_kernel(line_size, pieces, *refs):
    parts, sums = refs[:pieces], refs[pieces : 2 * pieces]
    core_bufs = refs[2 * pieces : 3 * pieces]
    pair_bufs = refs[3 * pieces : 4 * pieces]
    line_bufs = refs[4 * pieces : 5 * pieces]
    last_bufs = refs[5 * pieces : 6 * pieces]
    core_s, core_r, pair_s, pair_r, line_s, line_r, last_r, end_s, end_r = refs[6 * pieces :]
    replica, index, line, core = place()
    half = replica % 2
    to_core = {"fsdp": index + 1 - 2 * core}
    to_pair = {"replica": replica + 1 - 2 * half}
    right, left = {"fsdp": index + 2}, {"fsdp": index - 2}
    order = []
    for step in range((line_size + 1) // 2):
        order.append(line_size - 1 - step)
        if step != line_size - 1 - step:
            order.append(step)
    started = []

    def begin(condition, copy):
        if condition is None:
            copy.start()
        else:
            pl.when(condition)(copy.start)
        started.append((condition, copy))

    greet(replica, index, line, line_size, core)
    for s in order:
        for p in range(pieces):
            begin(
                None,
                remote(
                    parts[p].at[pl.ds(4 * s + 2 * (1 - core), 2)],
                    core_bufs[p].at[s],
                    core_s.at[s, p],
                    core_r.at[s, p],
                    to_core,
                ),
            )
    for s in order:
        for p in range(pieces):
            arrived = core_bufs[p].at[s]
            remote(arrived, arrived, core_s.at[s, p], core_r.at[s, p], to_core).wait_recv()
            core_bufs[p][s, 1 - half] = (
                core_bufs[p][s, 1 - half] + parts[p][4 * s + 2 * core + 1 - half]
            )
            begin(
                None,
                remote(
                    core_bufs[p].at[s, 1 - half],
                    pair_bufs[p].at[s],
                    pair_s.at[s, p],
                    pair_r.at[s, p],
                    to_pair,
                ),
            )
            core_bufs[p][s, half] = core_bufs[p][s, half] + parts[p][4 * s + 2 * core + half]
    for s in order:
        for p in range(pieces):
            arrived = pair_bufs[p].at[s]
            remote(arrived, arrived, pair_s.at[s, p], pair_r.at[s, p], to_pair).wait_recv()
            pair_bufs[p][s] = pair_bufs[p][s] + core_bufs[p][s, half]
            from_line = line_bufs[p].at[s]
            passes = jnp.logical_or(
                jnp.logical_and(line < s, line > 0),
                jnp.logical_and(line > s, line < line_size - 1),
            )

            @pl.when(passes)
            def _(s=s, p=p, from_line=from_line):
                remote(
                    from_line, from_line, line_s.at[s, p], line_r.at[s, p], right
                ).wait_recv()
                pair_bufs[p][s] = pair_bufs[p][s] + line_bufs[p][s]

            begin(
                line < s,
                remote(
                    pair_bufs[p].at[s], from_line, line_s.at[s, p], line_r.at[s, p], right
                ),
            )
            begin(
                line > s + 1,
                remote(pair_bufs[p].at[s], from_line, line_s.at[s, p], line_r.at[s, p], left),
            )
            begin(
                line == s + 1,
                remote(
                    pair_bufs[p].at[s], last_bufs[p], line_s.at[s, p], last_r.at[p], left
                ),
            )
    for s in order:

        @pl.when(line == s)
        def _(s=s):
            for p in range(pieces):
                if s > 0:
                    from_line = line_bufs[p].at[s]
                    remote(
                        from_line, from_line, line_s.at[s, p], line_r.at[s, p], right
                    ).wait_recv()
                    pair_bufs[p][s] = pair_bufs[p][s] + line_bufs[p][s]
                if s < line_size - 1:
                    last = last_bufs[p]
                    remote(last, last, line_s.at[s, p], last_r.at[p], left).wait_recv()
                    pair_bufs[p][s] = pair_bufs[p][s] + last[...]
                sums[p][half] = pair_bufs[p][s]
                remote(
                    sums[p].at[half], sums[p].at[half], end_s.at[p], end_r.at[p], to_pair
                ).start()

    for p in range(pieces):
        remote(
            sums[p].at[1 - half], sums[p].at[1 - half], end_s.at[p], end_r.at[p], to_pair
        ).wait_recv()
        remote(
            sums[p].at[half], sums[p].at[half], end_s.at[p], end_r.at[p], to_pair
        ).wait_send()
    for condition, copy in started:
        if condition is None:
            copy.wait_send()
        else:
            pl.when(condition)(copy.wait_send)


def reduce_parts(parts):
    size = lax.axis_size("fsdp")
    line_size = size // 2
    pieces = len(parts)
    split = [part.reshape(2 * size, -1, part.shape[1]) for part in parts]
    blocks = [part.shape[1:] for part in split]
    kind = jnp.bfloat16
    sums = pl.pallas_call(
        functools.partial(reduce_kernel, line_size, pieces),
        out_shape=[jax.ShapeDtypeStruct((2,) + block, kind) for block in blocks],
        in_specs=[pl.BlockSpec(memory_space=pltpu.VMEM)] * pieces,
        out_specs=[pl.BlockSpec(memory_space=pltpu.VMEM)] * pieces,
        scratch_shapes=[pltpu.VMEM((line_size, 2) + block, kind) for block in blocks]
        + [pltpu.VMEM((line_size,) + block, kind) for block in blocks]
        + [pltpu.VMEM((line_size,) + block, kind) for block in blocks]
        + [pltpu.VMEM(block, kind) for block in blocks]
        + [pltpu.SemaphoreType.DMA((line_size, pieces))] * 6
        + [pltpu.SemaphoreType.DMA((pieces,))] * 3,
        compiler_params=pltpu.CompilerParams(
            collective_id=1, has_side_effects=True, vmem_limit_bytes=vmem_bytes
        ),
    )(*split)
    return [total.reshape(-1, total.shape[2]) for total in sums]


def local(
    inputs,
    cotangent,
    norm_gains,
    head_gains,
    query_weight,
    key_weight,
    value_weight,
    out_weight,
    gate_weight,
    up_weight,
    down_weight,
):
    length = inputs.shape[0]
    devices = lax.axis_size("fsdp")
    rows = query_weight.shape[0]
    head_rows = head_gains.shape[1]
    small = jnp.concatenate(
        [norm_gains.T, jnp.pad(head_gains.T, ((0, rows - head_rows), (0, 0)))], axis=1
    )
    attention_shard = jnp.concatenate(
        [query_weight, key_weight, value_weight, out_weight.T, jnp.pad(small, ((0, 0), (0, 124)))],
        axis=1,
    )
    attention_full, gate_full, up_full, down_full = gather_shards(
        [attention_shard, gate_weight, up_weight, down_weight.T]
    )
    marks = [query_weight.shape[1], key_weight.shape[1], value_weight.shape[1], out_weight.shape[0]]
    marks = [sum(marks[: at + 1]) for at in range(4)]
    query_full = attention_full[:, : marks[0]]
    key_full = attention_full[:, marks[0] : marks[1]]
    value_full = attention_full[:, marks[1] : marks[2]]
    out_full = attention_full[:, marks[2] : marks[3]]
    gains_full = attention_full[:, marks[3] : marks[3] + 2].T
    heads_full = (
        attention_full[:, marks[3] + 2 : marks[3] + 4]
        .reshape(devices, rows, 2)[:, :head_rows]
        .reshape(HD, 2)
        .T
    )
    cosine_table, sine_table = rope_tables(length)
    local_heads = query_full.shape[1] // HD
    local_groups = key_full.shape[1] // HD
    group_size = local_heads // local_groups
    block_rows = min(length, 512)
    score_scale = 1.0 / math.sqrt(HD)
    residual_in = inputs.astype(jnp.float32)
    first_scale = inverse_rms(residual_in)
    first_hat = residual_in * first_scale
    first_gain = gains_full[0].astype(jnp.float32)
    first_low = (first_hat * first_gain).astype(jnp.bfloat16)
    query_raw = matmul(first_low, query_full).reshape(length, local_heads, HD)
    key_raw = matmul(first_low, key_full).reshape(length, local_groups, HD)
    value_low = matmul(first_low, value_full).astype(jnp.bfloat16).reshape(length, local_groups, HD)
    query_gain = heads_full[0].astype(jnp.float32)
    key_gain = heads_full[1].astype(jnp.float32)
    query_scale = inverse_rms(query_raw)
    query_hat = query_raw * query_scale
    query_low = rotate(query_hat * query_gain, cosine_table, sine_table).astype(jnp.bfloat16)
    query_low = query_low.reshape(length, local_groups, group_size, HD)
    key_scale = inverse_rms(key_raw)
    key_hat = key_raw * key_scale
    key_low = rotate(key_hat * key_gain, cosine_table, sine_table).astype(jnp.bfloat16)

    def masked_scores(block_start):
        key_span = block_start + block_rows
        scores = (
            jnp.einsum("qkgd,tkd->kgqt", query_low, key_low, preferred_element_type=jnp.float32)
            * score_scale
        )
        causal = (block_start + jnp.arange(block_rows))[:, None] >= jnp.arange(key_span)[None, :]
        return jnp.where(causal, scores, -1e30)

    block_index = 0
    block_start = block_index * block_rows
    masked = masked_scores(block_start)
    highest = jnp.max(masked, axis=-1, keepdims=True)
    powers = jnp.exp(masked - highest)
    totals = jnp.sum(powers, axis=-1, keepdims=True)
    softmax_low = (powers / totals).astype(jnp.bfloat16)
    log_totals = [highest + jnp.log(totals)]
    mixed_parts = jnp.einsum(
        "kgqt,tkd->qkgd", softmax_low, value_low, preferred_element_type=jnp.float32
    )
    mixed_low = mixed_parts.astype(jnp.bfloat16).reshape(length, local_heads * HD)
    attention_total = tensor_sum(cross_cols(mixed_low, out_full))
    hidden = residual_in + attention_total
    second_scale = inverse_rms(hidden)
    second_hat = hidden * second_scale
    second_gain = gains_full[1].astype(jnp.float32)
    second_low = (second_hat * second_gain).astype(jnp.bfloat16)
    gate_value = matmul(second_low, gate_full)
    up_value = matmul(second_low, up_full)
    sigmoid_gate = jax.nn.sigmoid(gate_value)
    swish = gate_value * sigmoid_gate
    inner_low = (swish * up_value).astype(jnp.bfloat16)
    swiglu_total = tensor_sum(cross_cols(inner_low, down_full))
    output = (hidden + swiglu_total).astype(jnp.bfloat16)
    grad_inner = matmul(cotangent, down_full)
    grad_gate = (
        grad_inner * up_value * sigmoid_gate * (1.0 + gate_value * (1.0 - sigmoid_gate))
    ).astype(jnp.bfloat16)
    grad_up = (grad_inner * swish).astype(jnp.bfloat16)
    grad_second = tensor_sum(cross_cols(grad_gate, gate_full) + cross_cols(grad_up, up_full))
    second_gain_grad = jnp.sum(grad_second * second_hat, axis=0)
    grad_hidden = cotangent.astype(jnp.float32) + norm_back(
        grad_second, second_hat, second_scale, second_gain
    )
    grad_hidden_low = grad_hidden.astype(jnp.bfloat16)
    out_part = cross_rows(grad_hidden_low, mixed_low)
    grad_mixed = (
        matmul(grad_hidden_low, out_full)
        .astype(jnp.bfloat16)
        .reshape(length, local_groups, group_size, HD)
    )
    grad_keys = jnp.zeros((length, local_groups, HD), jnp.float32)
    grad_values = jnp.zeros((length, local_groups, HD), jnp.float32)
    block_index = 0
    block_start = block_index * block_rows
    key_span = block_start + block_rows
    masked = masked_scores(block_start)
    powers = jnp.exp(masked - log_totals[block_index])
    grad_powers = jnp.einsum(
        "qkgd,tkd->kgqt", grad_mixed, value_low, preferred_element_type=jnp.float32
    )
    centred = jnp.sum(powers * grad_powers, axis=-1, keepdims=True)
    grad_scores = (powers * (grad_powers - centred)).astype(jnp.bfloat16)
    query_parts = (
        jnp.einsum("kgqt,tkd->qkgd", grad_scores, key_low, preferred_element_type=jnp.float32)
        * score_scale
    )
    grad_keys = grad_keys.at[:key_span].add(
        jnp.einsum("kgqt,qkgd->tkd", grad_scores, query_low, preferred_element_type=jnp.float32)
        * score_scale
    )
    grad_values = grad_values.at[:key_span].add(
        jnp.einsum(
            "kgqt,qkgd->tkd",
            powers.astype(jnp.bfloat16),
            grad_mixed,
            preferred_element_type=jnp.float32,
        )
    )
    grad_query_rot = query_parts.reshape(length, local_heads, HD)
    grad_query_gained = rotate(grad_query_rot, cosine_table, -sine_table)
    query_gain_grad = jnp.sum(grad_query_gained * query_hat, axis=(0, 1))
    grad_query = norm_back(grad_query_gained, query_hat, query_scale, query_gain).astype(
        jnp.bfloat16
    )
    grad_query = grad_query.reshape(length, local_heads * HD)
    grad_key_gained = rotate(grad_keys, cosine_table, -sine_table)
    key_gain_grad = jnp.sum(grad_key_gained * key_hat, axis=(0, 1))
    grad_key = norm_back(grad_key_gained, key_hat, key_scale, key_gain).astype(jnp.bfloat16)
    grad_key = grad_key.reshape(length, local_groups * HD)
    grad_value = grad_values.astype(jnp.bfloat16).reshape(length, local_groups * HD)
    query_part = cross_rows(first_low, grad_query)
    key_part = cross_rows(first_low, grad_key)
    value_part = cross_rows(first_low, grad_value)
    first_part = (
        cross_cols(grad_query, query_full)
        + cross_cols(grad_key, key_full)
        + cross_cols(grad_value, value_full)
    )
    grad_first = tensor_sum(first_part)
    head_part = tensor_sum(jnp.stack([query_gain_grad, key_gain_grad]))
    first_gain_grad = jnp.sum(grad_first * first_hat, axis=0)
    input_grad = (grad_hidden + norm_back(grad_first, first_hat, first_scale, first_gain)).astype(
        jnp.bfloat16
    )
    gains_part = jnp.stack([first_gain_grad, second_gain_grad])
    heads_part = jnp.pad(
        head_part.T.reshape(devices, head_rows, 2), ((0, 0), (0, rows - head_rows), (0, 0))
    ).reshape(devices * rows, 2)
    small_part = jnp.pad(jnp.concatenate([gains_part.T, heads_part], axis=1), ((0, 0), (0, 124)))
    attention_part = jnp.concatenate(
        [query_part, key_part, value_part, out_part, small_part], axis=1
    ).astype(jnp.bfloat16)
    summed = reduce_parts(
        [
            cross_rows(second_low, grad_gate).astype(jnp.bfloat16),
            cross_rows(second_low, grad_up).astype(jnp.bfloat16),
            cross_rows(cotangent, inner_low).astype(jnp.bfloat16),
            attention_part,
        ]
    )
    replicas = lax.axis_size("replica")
    if replicas > 2:
        summed = [lax.psum(total, "replica") * 0.5 for total in summed]
    gate_grad, up_grad, down_grad, attention_grad = [total.astype(jnp.float32) for total in summed]
    return (
        output,
        input_grad,
        attention_grad[:, marks[3] : marks[3] + 2].T,
        attention_grad[:head_rows, marks[3] + 2 : marks[3] + 4].T,
        attention_grad[:, : marks[0]],
        attention_grad[:, marks[0] : marks[1]],
        attention_grad[:, marks[1] : marks[2]],
        attention_grad[:, marks[2] : marks[3]].T,
        gate_grad,
        up_grad,
        down_grad.T,
    )


def solution(mesh):
    return jax.shard_map(
        local,
        mesh=mesh,
        in_specs=(
            P(("replica", "fsdp"), None),
            P(("replica", "fsdp"), None),
            P(None, "fsdp"),
            P(None, "fsdp"),
            P("fsdp", "tensor"),
            P("fsdp", "tensor"),
            P("fsdp", "tensor"),
            P("tensor", "fsdp"),
            P("fsdp", "tensor"),
            P("fsdp", "tensor"),
            P("tensor", "fsdp"),
        ),
        out_specs=(
            P(("replica", "fsdp"), None),
            P(("replica", "fsdp"), None),
            P(None, "fsdp"),
            P(None, "fsdp"),
            P("fsdp", "tensor"),
            P("fsdp", "tensor"),
            P("fsdp", "tensor"),
            P("tensor", "fsdp"),
            P("fsdp", "tensor"),
            P("fsdp", "tensor"),
            P("tensor", "fsdp"),
        ),
        check_vma=False,
    )
```

```python
import functools
import math

import jax
import jax.numpy as jnp
from jax import lax
from jax.experimental import pallas as pl
from jax.experimental.pallas import tpu as pltpu
from jax.sharding import PartitionSpec as P

HD = 64


epsilon = 1e-05
rope_base = 1000000.0


def inverse_rms(values):
    return lax.rsqrt(jnp.mean(values * values, axis=-1, keepdims=True) + epsilon)


def norm_back(grad_normed, normed, scaling, gain):
    scaled = grad_normed * gain
    return scaling * (scaled - normed * jnp.mean(scaled * normed, axis=-1, keepdims=True))


def rope_tables(length):
    half = HD // 2
    freqs = rope_base ** (-(jnp.arange(half, dtype=jnp.float32) * 2.0 / HD))
    angles = jnp.arange(length, dtype=jnp.float32)[:, None] * freqs[None, :]
    return (jnp.cos(angles)[:, None, :], jnp.sin(angles)[:, None, :])


def rotate(values, cosine_table, sine_table):
    half = values.shape[-1] // 2
    front = values[..., :half]
    behind = values[..., half:]
    return jnp.concatenate(
        [front * cosine_table - behind * sine_table, behind * cosine_table + front * sine_table],
        axis=-1,
    )


def matmul(left, right):
    return jnp.dot(left, right, preferred_element_type=jnp.float32)


def cross_rows(left, right):
    return lax.dot_general(
        left, right, (((0,), (0,)), ((), ())), preferred_element_type=jnp.float32
    )


def cross_cols(left, right):
    return lax.dot_general(
        left, right, (((1,), (1,)), ((), ())), preferred_element_type=jnp.float32
    )


MESH = pl.DeviceIdType.MESH
vmem_bytes = 60 * 1024 * 1024


def place():
    replica = lax.axis_index("replica")
    index = lax.axis_index("fsdp")
    return replica, index, index // 2, index % 2


def greet(replica, index, line, line_size, core):
    barrier = pltpu.get_barrier_semaphore()
    other_core = index + 1 - 2 * core
    other_replica = replica + 1 - 2 * (replica % 2)
    pl.semaphore_signal(barrier, inc=1, device_id={"fsdp": other_core}, device_id_type=MESH)
    pl.semaphore_signal(barrier, inc=1, device_id={"replica": other_replica}, device_id_type=MESH)

    @pl.when(line < line_size - 1)
    def _():
        pl.semaphore_signal(barrier, inc=1, device_id={"fsdp": index + 2}, device_id_type=MESH)

    @pl.when(line > 0)
    def _():
        pl.semaphore_signal(barrier, inc=1, device_id={"fsdp": index - 2}, device_id_type=MESH)

    ends = (line == 0).astype(jnp.int32) + (line == line_size - 1).astype(jnp.int32)
    pl.semaphore_wait(barrier, 4 - ends)


def remote(source, target, send, receive, where):
    return pltpu.make_async_remote_copy(
        src_ref=source,
        dst_ref=target,
        send_sem=send,
        recv_sem=receive,
        device_id=where,
        device_id_type=MESH,
    )


def pair_permute(values, axis):
    return lax.ppermute(values, axis, [(at, at ^ 1) for at in range(lax.axis_size(axis))])


def tensor_sum(values):
    low = values.astype(jnp.bfloat16)
    if lax.axis_size("tensor") != 2:
        return lax.psum(low.astype(jnp.float32), "tensor")
    other = pair_permute(low, "tensor")
    return low.astype(jnp.float32) + other.astype(jnp.float32)


def gather_kernel(line_size, pieces, *refs):
    shards, wholes, sems = refs[:pieces], refs[pieces : 2 * pieces], refs[2 * pieces :]
    own_sem, core_s, core_r, line_s, line_r, pair_s, pair_r, one_s, one_r, two_s, two_r = sems
    replica, index, line, core = place()
    half = replica % 2
    to_core = {"fsdp": index + 1 - 2 * core}
    to_pair = {"replica": replica + 1 - 2 * half}
    neighbours = ({"fsdp": index + 2}, {"fsdp": index - 2})
    may_send = (line < line_size - 1, line > 0)
    started = []

    def begin(condition, copy):
        if condition is None:
            copy.start()
        else:
            pl.when(condition)(copy.start)
        started.append((condition, copy))

    def slot(position, which_core, which_half):
        return 4 * position + 2 * which_core + which_half

    greet(replica, index, line, line_size, core)
    own_copies = []
    for p in range(pieces):
        for way in range(2):
            begin(
                may_send[way],
                remote(
                    shards[p].at[half],
                    wholes[p].at[slot(line, core, half)],
                    line_s.at[way, 0, p],
                    line_r.at[way, 0, p],
                    neighbours[way],
                ),
            )
    for p in range(pieces):
        target = wholes[p].at[pl.ds(2 * index, 2)]
        begin(None, remote(shards[p], target, core_s.at[p], core_r.at[p], to_core))
        copy = pltpu.make_async_copy(shards[p], target, own_sem.at[p])
        copy.start()
        own_copies.append(copy)

    def source_of(way, hop):
        position = line - hop if way == 0 else line + hop
        return position, (position >= 0 if way == 0 else position <= line_size - 1)

    def spread(hop):
        for p in range(pieces):
            for way in range(2):
                position, present = source_of(way, hop)
                place_here = wholes[p].at[slot(position, core, 1 - half)]
                arrival = remote(
                    place_here,
                    place_here,
                    pair_s.at[way, hop - 1, p],
                    pair_r.at[way, hop - 1, p],
                    to_pair,
                )
                pl.when(present)(arrival.wait_recv)
                begin(
                    present,
                    remote(
                        place_here,
                        place_here,
                        two_s.at[way, hop - 1, p],
                        two_r.at[way, hop - 1, p],
                        to_core,
                    ),
                )

    for hop in range(1, line_size):
        for p in range(pieces):
            for way in range(2):
                position, present = source_of(way, hop)
                block = wholes[p].at[slot(position, core, half)]
                arrival = remote(
                    block,
                    block,
                    line_s.at[way, hop - 1, p],
                    line_r.at[way, hop - 1, p],
                    neighbours[way],
                )
                pl.when(present)(arrival.wait_recv)
                if hop < line_size - 1:
                    begin(
                        jnp.logical_and(present, may_send[way]),
                        remote(
                            block,
                            block,
                            line_s.at[way, hop, p],
                            line_r.at[way, hop, p],
                            neighbours[way],
                        ),
                    )
                begin(
                    present,
                    remote(
                        block,
                        block,
                        pair_s.at[way, hop - 1, p],
                        pair_r.at[way, hop - 1, p],
                        to_pair,
                    ),
                )
                begin(
                    present,
                    remote(
                        block,
                        block,
                        one_s.at[way, hop - 1, p],
                        one_r.at[way, hop - 1, p],
                        to_core,
                    ),
                )
        if hop > 1:
            spread(hop - 1)
    spread(line_size - 1)
    for p in range(pieces):
        own_copies[p].wait()
        target = wholes[p].at[pl.ds(2 * (index + 1 - 2 * core), 2)]
        remote(target, target, core_s.at[p], core_r.at[p], to_core).wait_recv()
        for hop in range(1, line_size):
            for way in range(2):
                position, present = source_of(way, hop)
                first = wholes[p].at[slot(position, 1 - core, half)]
                second = wholes[p].at[slot(position, 1 - core, 1 - half)]
                sems_at = (way, hop - 1, p)
                pl.when(present)(
                    remote(first, first, one_s.at[sems_at], one_r.at[sems_at], to_core).wait_recv
                )
                pl.when(present)(
                    remote(second, second, two_s.at[sems_at], two_r.at[sems_at], to_core).wait_recv
                )
    for condition, copy in started:
        if condition is None:
            copy.wait_send()
        else:
            pl.when(condition)(copy.wait_send)


def gather_shards(shards):
    size = lax.axis_size("fsdp")
    line_size = size // 2
    pieces = len(shards)
    split = [shard.reshape(2, shard.shape[0] // 2, shard.shape[1]) for shard in shards]
    hops = (2, line_size - 1, pieces)
    wholes = pl.pallas_call(
        functools.partial(gather_kernel, line_size, pieces),
        out_shape=[
            jax.ShapeDtypeStruct((2 * size,) + shard.shape[1:], shard.dtype) for shard in split
        ],
        in_specs=[pl.BlockSpec(memory_space=pl.ANY)] * pieces,
        out_specs=[pl.BlockSpec(memory_space=pl.ANY)] * pieces,
        scratch_shapes=[pltpu.SemaphoreType.DMA((pieces,))] * 3
        + [pltpu.SemaphoreType.DMA(hops)] * 8,
        compiler_params=pltpu.CompilerParams(
            collective_id=0, has_side_effects=True, vmem_limit_bytes=vmem_bytes
        ),
    )(*split)
    return [whole.reshape(-1, whole.shape[2]) for whole in wholes]


def reduce_kernel(line_size, early, pieces, *refs):
    late = pieces - early
    parts, sums = refs[:pieces], refs[pieces : 2 * pieces]
    line_bufs = refs[2 * pieces : 3 * pieces]
    last_bufs = refs[3 * pieces : 4 * pieces]
    core_bufs = refs[4 * pieces : 4 * pieces + late]
    pair_bufs = refs[4 * pieces + late : 4 * pieces + 2 * late]
    core_s, core_r, pair_s, pair_r, line_s, line_r, last_r, end_s, end_r = refs[
        4 * pieces + 2 * late :
    ]
    replica, index, line, core = place()
    half = replica % 2
    to_core = {"fsdp": index + 1 - 2 * core}
    to_pair = {"replica": replica + 1 - 2 * half}
    right, left = {"fsdp": index + 2}, {"fsdp": index - 2}
    order = []
    for step in range((line_size + 1) // 2):
        order.append(line_size - 1 - step)
        if step != line_size - 1 - step:
            order.append(step)
    started = []

    def begin(condition, copy):
        if condition is None:
            copy.start()
        else:
            pl.when(condition)(copy.start)
        started.append((condition, copy))

    def own_of(p):
        return parts[p] if p < early else pair_bufs[p - early]

    def meet_cores():
        for s in order:
            for q in range(late):
                full = parts[early + q]
                arrived = core_bufs[q].at[s]
                remote(arrived, arrived, core_s.at[s, q], core_r.at[s, q], to_core).wait_recv()
                core_bufs[q][s, 1 - half] = (
                    core_bufs[q][s, 1 - half] + full[4 * s + 2 * core + 1 - half]
                )
                begin(
                    None,
                    remote(
                        core_bufs[q].at[s, 1 - half],
                        pair_bufs[q].at[s],
                        pair_s.at[s, q],
                        pair_r.at[s, q],
                        to_pair,
                    ),
                )
                core_bufs[q][s, half] = core_bufs[q][s, half] + full[4 * s + 2 * core + half]

    def along(s, p):
        own, running = own_of(p), line_bufs[p]
        if p >= early:
            q = p - early
            arrived = own.at[s]
            remote(arrived, arrived, pair_s.at[s, q], pair_r.at[s, q], to_pair).wait_recv()
            own[s] = own[s] + core_bufs[q][s, half]
        opens = jnp.logical_or(
            jnp.logical_and(line == 0, line < s),
            jnp.logical_and(line == line_size - 1, line > s),
        )
        passes = jnp.logical_or(
            jnp.logical_and(line > 0, line < s),
            jnp.logical_and(line < line_size - 1, line > s),
        )

        @pl.when(passes)
        def _():
            arrived = running.at[s]
            remote(arrived, arrived, line_s.at[s, p], line_r.at[s, p], right).wait_recv()
            running[s] = running[s] + own[s]

        for condition, source in ((opens, own), (passes, running)):
            begin(
                jnp.logical_and(condition, line < s),
                remote(source.at[s], running.at[s], line_s.at[s, p], line_r.at[s, p], right),
            )
            begin(
                jnp.logical_and(condition, line > s + 1),
                remote(source.at[s], running.at[s], line_s.at[s, p], line_r.at[s, p], left),
            )
            begin(
                jnp.logical_and(condition, line == s + 1),
                remote(source.at[s], last_bufs[p], line_s.at[s, p], last_r.at[p], left),
            )

    def end(s, p):
        @pl.when(line == s)
        def _():
            total = own_of(p)[s]
            if s > 0:
                arrived = line_bufs[p].at[s]
                remote(arrived, arrived, line_s.at[s, p], line_r.at[s, p], right).wait_recv()
                total = total + line_bufs[p][s]
            if s < line_size - 1:
                last = last_bufs[p]
                remote(last, last, line_s.at[s, p], last_r.at[p], left).wait_recv()
                total = total + last[...]
            sums[p][half] = total
            remote(
                sums[p].at[half], sums[p].at[half], end_s.at[p], end_r.at[p], to_pair
            ).start()

    greet(replica, index, line, line_size, core)
    for s in order:
        for q in range(late):
            begin(
                None,
                remote(
                    parts[early + q].at[pl.ds(4 * s + 2 * (1 - core), 2)],
                    core_bufs[q].at[s],
                    core_s.at[s, q],
                    core_r.at[s, q],
                    to_core,
                ),
            )
    if early:
        along(order[0], 0)
    meet_cores()
    for group in (range(early), range(early, pieces)):
        for at, s in enumerate(order):
            for p in group:
                if at > 0 or p > 0:
                    along(s, p)
            if at > 0:
                for p in group:
                    end(order[at - 1], p)
        for p in group:
            end(order[-1], p)
    for p in range(pieces):
        remote(
            sums[p].at[1 - half], sums[p].at[1 - half], end_s.at[p], end_r.at[p], to_pair
        ).wait_recv()
        remote(
            sums[p].at[half], sums[p].at[half], end_s.at[p], end_r.at[p], to_pair
        ).wait_send()
    for condition, copy in started:
        if condition is None:
            copy.wait_send()
        else:
            pl.when(condition)(copy.wait_send)


def meeting_order(size, rows):
    core, half = lax.axis_index("fsdp") % 2, lax.axis_index("replica") % 2
    line_size, half_rows = size // 2, rows // 2
    at = jnp.arange(size * rows)
    row, position = at % half_rows, (at // half_rows) % line_size
    own_half, own_core = (at // (half_rows * line_size)) % 2, at // (2 * half_rows * line_size)
    from_core = jnp.where(own_core == 1, core, 1 - core)
    from_half = jnp.where(own_half == 1, half, 1 - half)
    source = ((2 * position + from_core) * 2 + from_half) * half_rows + row
    return (jnp.arange(size * rows)[:, None] == source[None, :]).astype(jnp.bfloat16)


def meet(left, right):
    middle = left.shape[1] // 2
    sent = cross_rows(left[:, :middle], right).astype(jnp.bfloat16)
    other_core = pair_permute(sent, "fsdp").astype(jnp.float32)
    mine = (cross_rows(left[:, middle:], right) + other_core).astype(jnp.bfloat16)
    other_pair = pair_permute(mine[: middle // 2], "replica")
    both = mine[middle // 2 :].astype(jnp.float32) + other_pair.astype(jnp.float32)
    return both.astype(jnp.bfloat16)


def reduce_parts(met, parts):
    size = lax.axis_size("fsdp")
    line_size = size // 2
    early, late = len(met), len(parts)
    pieces = early + late
    split = [part.reshape(line_size, -1, part.shape[1]) for part in met]
    split += [part.reshape(2 * size, -1, part.shape[1]) for part in parts]
    blocks = [part.shape[1:] for part in split]
    kind = jnp.bfloat16
    sums = pl.pallas_call(
        functools.partial(reduce_kernel, line_size, early, pieces),
        out_shape=[jax.ShapeDtypeStruct((2,) + block, kind) for block in blocks],
        in_specs=[pl.BlockSpec(memory_space=pltpu.VMEM)] * pieces,
        out_specs=[pl.BlockSpec(memory_space=pltpu.VMEM)] * pieces,
        scratch_shapes=[pltpu.VMEM((line_size,) + block, kind) for block in blocks]
        + [pltpu.VMEM(block, kind) for block in blocks]
        + [pltpu.VMEM((line_size, 2) + block, kind) for block in blocks[early:]]
        + [pltpu.VMEM((line_size,) + block, kind) for block in blocks[early:]]
        + [pltpu.SemaphoreType.DMA((line_size, late))] * 4
        + [pltpu.SemaphoreType.DMA((line_size, pieces))] * 2
        + [pltpu.SemaphoreType.DMA((pieces,))] * 3,
        compiler_params=pltpu.CompilerParams(
            collective_id=1, has_side_effects=True, vmem_limit_bytes=vmem_bytes
        ),
    )(*split)
    return [total.reshape(-1, total.shape[2]) for total in sums]


def local(
    inputs,
    cotangent,
    norm_gains,
    head_gains,
    query_weight,
    key_weight,
    value_weight,
    out_weight,
    gate_weight,
    up_weight,
    down_weight,
):
    length = inputs.shape[0]
    devices = lax.axis_size("fsdp")
    rows = query_weight.shape[0]
    head_rows = head_gains.shape[1]
    small = jnp.concatenate(
        [norm_gains.T, jnp.pad(head_gains.T, ((0, rows - head_rows), (0, 0)))], axis=1
    )
    attention_shard = jnp.concatenate(
        [query_weight, key_weight, value_weight, out_weight.T, jnp.pad(small, ((0, 0), (0, 124)))],
        axis=1,
    )
    attention_full, gate_full, up_full, down_full = gather_shards(
        [attention_shard, gate_weight, up_weight, down_weight.T]
    )
    marks = [query_weight.shape[1], key_weight.shape[1], value_weight.shape[1], out_weight.shape[0]]
    marks = [sum(marks[: at + 1]) for at in range(4)]
    query_full = attention_full[:, : marks[0]]
    key_full = attention_full[:, marks[0] : marks[1]]
    value_full = attention_full[:, marks[1] : marks[2]]
    out_full = attention_full[:, marks[2] : marks[3]]
    gains_full = attention_full[:, marks[3] : marks[3] + 2].T
    heads_full = (
        attention_full[:, marks[3] + 2 : marks[3] + 4]
        .reshape(devices, rows, 2)[:, :head_rows]
        .reshape(HD, 2)
        .T
    )
    cosine_table, sine_table = rope_tables(length)
    local_heads = query_full.shape[1] // HD
    local_groups = key_full.shape[1] // HD
    group_size = local_heads // local_groups
    block_rows = min(length, 512)
    score_scale = 1.0 / math.sqrt(HD)
    residual_in = inputs.astype(jnp.float32)
    first_scale = inverse_rms(residual_in)
    first_hat = residual_in * first_scale
    first_gain = gains_full[0].astype(jnp.float32)
    first_low = (first_hat * first_gain).astype(jnp.bfloat16)
    query_raw = matmul(first_low, query_full).reshape(length, local_heads, HD)
    key_raw = matmul(first_low, key_full).reshape(length, local_groups, HD)
    value_low = matmul(first_low, value_full).astype(jnp.bfloat16).reshape(length, local_groups, HD)
    query_gain = heads_full[0].astype(jnp.float32)
    key_gain = heads_full[1].astype(jnp.float32)
    query_scale = inverse_rms(query_raw)
    query_hat = query_raw * query_scale
    query_low = rotate(query_hat * query_gain, cosine_table, sine_table).astype(jnp.bfloat16)
    query_low = query_low.reshape(length, local_groups, group_size, HD)
    key_scale = inverse_rms(key_raw)
    key_hat = key_raw * key_scale
    key_low = rotate(key_hat * key_gain, cosine_table, sine_table).astype(jnp.bfloat16)

    def masked_scores(block_start):
        key_span = block_start + block_rows
        scores = (
            jnp.einsum("qkgd,tkd->kgqt", query_low, key_low, preferred_element_type=jnp.float32)
            * score_scale
        )
        causal = (block_start + jnp.arange(block_rows))[:, None] >= jnp.arange(key_span)[None, :]
        return jnp.where(causal, scores, -1e30)

    block_index = 0
    block_start = block_index * block_rows
    masked = masked_scores(block_start)
    highest = jnp.max(masked, axis=-1, keepdims=True)
    powers = jnp.exp(masked - highest)
    totals = jnp.sum(powers, axis=-1, keepdims=True)
    softmax_low = (powers / totals).astype(jnp.bfloat16)
    log_totals = [highest + jnp.log(totals)]
    mixed_parts = jnp.einsum(
        "kgqt,tkd->qkgd", softmax_low, value_low, preferred_element_type=jnp.float32
    )
    mixed_low = mixed_parts.astype(jnp.bfloat16).reshape(length, local_heads * HD)
    attention_total = tensor_sum(cross_cols(mixed_low, out_full))
    hidden = residual_in + attention_total
    second_scale = inverse_rms(hidden)
    second_hat = hidden * second_scale
    second_gain = gains_full[1].astype(jnp.float32)
    second_low = (second_hat * second_gain).astype(jnp.bfloat16)
    gate_value = matmul(second_low, gate_full)
    up_value = matmul(second_low, up_full)
    sigmoid_gate = jax.nn.sigmoid(gate_value)
    swish = gate_value * sigmoid_gate
    inner_low = (swish * up_value).astype(jnp.bfloat16)
    swiglu_total = tensor_sum(cross_cols(inner_low, down_full))
    output = (hidden + swiglu_total).astype(jnp.bfloat16)
    swap = meeting_order(devices, rows)
    down_met = meet(matmul(cotangent, swap).astype(jnp.bfloat16), inner_low)
    grad_inner = matmul(cotangent, down_full)
    grad_gate = (
        grad_inner * up_value * sigmoid_gate * (1.0 + gate_value * (1.0 - sigmoid_gate))
    ).astype(jnp.bfloat16)
    grad_up = (grad_inner * swish).astype(jnp.bfloat16)
    second_swapped = matmul(second_low, swap).astype(jnp.bfloat16)
    gate_met = meet(second_swapped, grad_gate)
    up_met = meet(second_swapped, grad_up)
    grad_second = tensor_sum(cross_cols(grad_gate, gate_full) + cross_cols(grad_up, up_full))
    second_gain_grad = jnp.sum(grad_second * second_hat, axis=0)
    grad_hidden = cotangent.astype(jnp.float32) + norm_back(
        grad_second, second_hat, second_scale, second_gain
    )
    grad_hidden_low = grad_hidden.astype(jnp.bfloat16)
    out_part = cross_rows(grad_hidden_low, mixed_low)
    grad_mixed = (
        matmul(grad_hidden_low, out_full)
        .astype(jnp.bfloat16)
        .reshape(length, local_groups, group_size, HD)
    )
    grad_keys = jnp.zeros((length, local_groups, HD), jnp.float32)
    grad_values = jnp.zeros((length, local_groups, HD), jnp.float32)
    block_index = 0
    block_start = block_index * block_rows
    key_span = block_start + block_rows
    masked = masked_scores(block_start)
    powers = jnp.exp(masked - log_totals[block_index])
    grad_powers = jnp.einsum(
        "qkgd,tkd->kgqt", grad_mixed, value_low, preferred_element_type=jnp.float32
    )
    centred = jnp.sum(powers * grad_powers, axis=-1, keepdims=True)
    grad_scores = (powers * (grad_powers - centred)).astype(jnp.bfloat16)
    query_parts = (
        jnp.einsum("kgqt,tkd->qkgd", grad_scores, key_low, preferred_element_type=jnp.float32)
        * score_scale
    )
    grad_keys = grad_keys.at[:key_span].add(
        jnp.einsum("kgqt,qkgd->tkd", grad_scores, query_low, preferred_element_type=jnp.float32)
        * score_scale
    )
    grad_values = grad_values.at[:key_span].add(
        jnp.einsum(
            "kgqt,qkgd->tkd",
            powers.astype(jnp.bfloat16),
            grad_mixed,
            preferred_element_type=jnp.float32,
        )
    )
    grad_query_rot = query_parts.reshape(length, local_heads, HD)
    grad_query_gained = rotate(grad_query_rot, cosine_table, -sine_table)
    query_gain_grad = jnp.sum(grad_query_gained * query_hat, axis=(0, 1))
    grad_query = norm_back(grad_query_gained, query_hat, query_scale, query_gain).astype(
        jnp.bfloat16
    )
    grad_query = grad_query.reshape(length, local_heads * HD)
    grad_key_gained = rotate(grad_keys, cosine_table, -sine_table)
    key_gain_grad = jnp.sum(grad_key_gained * key_hat, axis=(0, 1))
    grad_key = norm_back(grad_key_gained, key_hat, key_scale, key_gain).astype(jnp.bfloat16)
    grad_key = grad_key.reshape(length, local_groups * HD)
    grad_value = grad_values.astype(jnp.bfloat16).reshape(length, local_groups * HD)
    query_part = cross_rows(first_low, grad_query)
    key_part = cross_rows(first_low, grad_key)
    value_part = cross_rows(first_low, grad_value)
    first_part = (
        cross_cols(grad_query, query_full)
        + cross_cols(grad_key, key_full)
        + cross_cols(grad_value, value_full)
    )
    grad_first = tensor_sum(first_part)
    head_part = tensor_sum(jnp.stack([query_gain_grad, key_gain_grad]))
    first_gain_grad = jnp.sum(grad_first * first_hat, axis=0)
    input_grad = (grad_hidden + norm_back(grad_first, first_hat, first_scale, first_gain)).astype(
        jnp.bfloat16
    )
    gains_part = jnp.stack([first_gain_grad, second_gain_grad])
    heads_part = jnp.pad(
        head_part.T.reshape(devices, head_rows, 2), ((0, 0), (0, rows - head_rows), (0, 0))
    ).reshape(devices * rows, 2)
    small_part = jnp.pad(jnp.concatenate([gains_part.T, heads_part], axis=1), ((0, 0), (0, 124)))
    attention_part = jnp.concatenate(
        [query_part, key_part, value_part, out_part, small_part], axis=1
    ).astype(jnp.bfloat16)
    summed = reduce_parts([gate_met, up_met, down_met], [attention_part])
    replicas = lax.axis_size("replica")
    if replicas > 2:
        summed = [lax.psum(total, "replica") * 0.5 for total in summed]
    gate_grad, up_grad, down_grad, attention_grad = [total.astype(jnp.float32) for total in summed]
    return (
        output,
        input_grad,
        attention_grad[:, marks[3] : marks[3] + 2].T,
        attention_grad[:head_rows, marks[3] + 2 : marks[3] + 4].T,
        attention_grad[:, : marks[0]],
        attention_grad[:, marks[0] : marks[1]],
        attention_grad[:, marks[1] : marks[2]],
        attention_grad[:, marks[2] : marks[3]].T,
        gate_grad,
        up_grad,
        down_grad.T,
    )


def solution(mesh):
    return jax.shard_map(
        local,
        mesh=mesh,
        in_specs=(
            P(("replica", "fsdp"), None),
            P(("replica", "fsdp"), None),
            P(None, "fsdp"),
            P(None, "fsdp"),
            P("fsdp", "tensor"),
            P("fsdp", "tensor"),
            P("fsdp", "tensor"),
            P("tensor", "fsdp"),
            P("fsdp", "tensor"),
            P("fsdp", "tensor"),
            P("tensor", "fsdp"),
        ),
        out_specs=(
            P(("replica", "fsdp"), None),
            P(("replica", "fsdp"), None),
            P(None, "fsdp"),
            P(None, "fsdp"),
            P("fsdp", "tensor"),
            P("fsdp", "tensor"),
            P("fsdp", "tensor"),
            P("tensor", "fsdp"),
            P("fsdp", "tensor"),
            P("fsdp", "tensor"),
            P("tensor", "fsdp"),
        ),
        check_vma=False,
    )
```
